1024 devices in a mesh: comp: 2 (over x_hi), row: 32 (over x_lo, y, core), col: 16 (over z).
Axes of the slice: x: 4 (x_hi: 2, x_lo: 2; x = x_hi * 2 + x_lo), y: 8, z: 16, core: 2. Of those that a mesh axis runs over, the one named last changes fastest.
Arguments:
- model_state: float32 [2, 1280, 32, 2048], P('comp', 'row', None, 'col'), may hold values from -6 to 6
- legendre: bfloat16 [32, 1280, 1280], P('row'), may hold values from -0.15625 to 0.15625
- gauss_weight: float32 [1280], P('row'), may hold values from 0.5 to 1.5
- mixing: float32 [32, 32], replicated, may hold values from -1 to 1
- surface: float32 [2, 1280, 2048], P('comp', 'row', 'col'), may hold values from -6 to 6
- sea_count: int32 [2, 1280, 16], P('comp', 'row', 'col'), may hold values from 0 to 128, as said below
- remap_source: int32 [2, 1280, 2048], P('comp', 'row', 'col'), may hold values from 0 to 5119
Outputs:
- new_state: float32 [2, 1280, 32, 2048], P('comp', 'row', None, 'col')
- new_surface: float32 [2, 1280, 2048], P('comp', 'row', 'col')
The draws below stay inside these ranges and needn't reach their ends.
Inputs may be any that keep to these rules, and one draw needn't show every extreme that they name: `sea_count`: the sea cells of a tile row are its first ones, of 128. `remap_source`: an entry counts row-major within a tile of 40 rows and 128 columns.
All inputs are finite; a program needn't handle non-finite values.
Results may differ from the reference program's by a relative error of at most 0.0043.
Values may be sent and summed in bfloat16 or wider, within the bound.
A program may use at most 32 MiB of HBM per device.

```python
import jax
import jax.numpy as jnp
from jax import lax

ROWS = 1280
NWAVE = 1280
WAVES = 32
COL_DEV = 128
LAT_DEV = 40
COLS = 2048
N_ROW = 32
N_COL = 16


def draw_sea_count(key, part):
    toss_key = jax.random.fold_in(key, 11)
    count_key = jax.random.fold_in(key, 12)
    coin_toss = jax.random.randint(toss_key, (2, ROWS, N_COL), 0, 16)
    partial_count = jax.random.randint(count_key, (2, ROWS, N_COL), 0, COL_DEV + 1)
    return jnp.where(coin_toss < 15, COL_DEV, partial_count).astype(jnp.int32)


def place_ends(array, key, low, high):
    longest = array.shape.index(max(array.shape))
    spots = []
    for shift in (0, 1):
        where = [jax.random.randint(jax.random.fold_in(key, axis), (), 0, length) for axis, length in enumerate(array.shape)]
        where[longest] = (where[longest] + shift) % array.shape[longest]
        spots.append(tuple(where))
    return array.at[spots[0]].set(low).at[spots[1]].set(high)


def block_levels(rng, dims, shards, least, largest):
    def one(dim, shards_of):
        heights = jax.random.uniform(jax.random.fold_in(jax.random.fold_in(rng, 6), dim), (shards_of,), jnp.float32, least / len(shards), largest / len(shards))
        return jnp.repeat(jnp.exp(heights), dims[dim] // shards_of).reshape((-1,) + (1,) * (len(dims) - dim - 1))

    loudness = one(*shards[0])
    for cut in shards[1:]:
        loudness = loudness * one(*cut)
    return loudness


def gaussian(own_key, shape, width, reach, pieces=(), dtype=jnp.bfloat16):
    drawn = width * jax.random.normal(own_key, shape, jnp.float32)
    if pieces:
        drawn = drawn * block_levels(own_key, shape, pieces, -0.22, 0.18)
    return jnp.clip(drawn, -reach, reach).astype(dtype)


def setup_inputs(seed: int = 0) -> dict:
    splits = jax.random.split(jax.random.key(seed), 8)
    return {
        "model_state": gaussian(splits[0], (2, ROWS, WAVES, COLS), 1.0, 6.0, ((0, 2), (1, 32), (3, 16)), jnp.float32),
        "legendre": gaussian(splits[1], (WAVES, ROWS, NWAVE), ROWS ** -0.5, 0.15625, ((0, 32),)),
        "gauss_weight": jnp.clip(0.5 + 1.0 * jax.random.uniform(splits[2], (ROWS,), jnp.float32) ** block_levels(splits[2], (ROWS,), ((0, 32),), -0.2, 0.2), 0.5, 1.5),
        "mixing": gaussian(splits[3], (WAVES, WAVES), WAVES ** -0.5, 1.0, (), jnp.float32),
        "surface": gaussian(splits[4], (2, ROWS, COLS), 1.0, 6.0, ((0, 2), (1, 32), (2, 16)), jnp.float32),
        "sea_count": draw_sea_count(jax.random.fold_in(splits[7], 71), 0),
        "remap_source": place_ends(jax.random.randint(splits[6], (2, ROWS, COLS), 0, LAT_DEV * COL_DEV), jax.random.fold_in(splits[6], 1), 0, (LAT_DEV * COL_DEV) - 1).astype(jnp.int32),
    }


def damping_rows(wave_count, nwave_count):
    total_wave = (jnp.arange(wave_count)[:, None] + jnp.arange(nwave_count)[None, :]).astype(jnp.float32)
    wave_ratio = total_wave * (total_wave + 1.0) / (1279.0 * 1280.0)
    return 1.0 / (1.0 + 20.0 * wave_ratio * wave_ratio)


def atmosphere(fourier, gauss_weight, legendre):
    weighted = (gauss_weight[:, None, None] * fourier).astype(jnp.bfloat16)
    damping = damping_rows(WAVES, NWAVE)

    def one_wave(spectral_mode):
        legendre_rows = legendre[spectral_mode]
        column = lax.dynamic_index_in_dim(weighted, spectral_mode, 1, keepdims=False)
        spectral = jnp.dot(legendre_rows.T, column, preferred_element_type=jnp.float32)
        filtered = (damping[spectral_mode][:, None] * spectral).astype(jnp.bfloat16)
        return jnp.dot(legendre_rows, filtered, preferred_element_type=jnp.float32).astype(jnp.bfloat16)

    synthesized = lax.map(one_wave, jnp.arange(WAVES).astype(jnp.int32))
    return jnp.transpose(synthesized, (1, 0, 2)).astype(jnp.float32)


def laplace(field):
    padded = jnp.pad(field, ((1, 1), (1, 1)))
    centre = padded[1:-1, 1:-1]
    return padded[2:, 1:-1] + padded[:-2, 1:-1] + padded[1:-1, 2:] + padded[1:-1, :-2] - 4.0 * centre


def diffuse(level_field, water_mask):
    first_step = level_field + 0.2 * water_mask * laplace(water_mask * level_field)
    return first_step + 0.2 * water_mask * laplace(water_mask * first_step)


def advance_ocean(heat_level, mixing, water_mask):
    blended_field = heat_level + water_mask[:, None, :] * jnp.einsum("do,eot->edt", mixing, heat_level, precision=lax.Precision.HIGHEST)

    def one_level(level_index):
        return diffuse(lax.dynamic_index_in_dim(blended_field, level_index, 1, keepdims=False), water_mask)

    levels = lax.map(one_level, jnp.arange(WAVES).astype(jnp.int32))
    return jnp.transpose(levels, (1, 0, 2))


def sea_cells(counts):
    position = jnp.arange(COLS) % COL_DEV
    block_index = jnp.arange(COLS) // COL_DEV
    return (position[None, :] < counts[:, block_index]).astype(jnp.float32)


def split_into_patches(field):
    return field.reshape(N_ROW, LAT_DEV, N_COL, COL_DEV).transpose(0, 2, 1, 3).reshape(N_ROW, N_COL, LAT_DEV * COL_DEV)


def pull_partner(other, source):
    pulled = jnp.take_along_axis(split_into_patches(other), split_into_patches(source), axis=2)
    return pulled.reshape(N_ROW, N_COL, LAT_DEV, COL_DEV).transpose(0, 2, 1, 3).reshape(ROWS, COLS)


def reference(model_state, legendre, gauss_weight, mixing, surface, sea_count, remap_source):
    sea_air = sea_cells(sea_count[0])
    sea_ocean = sea_cells(sea_count[1])
    synthesized = atmosphere(model_state[0], gauss_weight, legendre)
    ocean_state = advance_ocean(model_state[1], mixing, sea_ocean)
    gap_air = sea_air * (pull_partner(surface[1], remap_source[0]) - surface[0])
    gap_ocean = sea_ocean * (pull_partner(surface[0], remap_source[1]) - surface[1])
    new_surface = jnp.stack([surface[0] + 0.5 * gap_air, surface[1] + 0.25 * gap_ocean])
    ocean_state = ocean_state.at[:, 0, :].add(0.3 * gap_ocean)
    new_state = jnp.stack([synthesized, ocean_state])
    return new_state, new_surface
```

```python
import functools

import jax
import jax.numpy as jnp
from jax import lax
from jax.experimental import pallas as pl
from jax.experimental.pallas import tpu as pltpu
from jax.sharding import PartitionSpec as P

MESH = pl.DeviceIdType.MESH
F32 = jnp.float32
BF16 = jnp.bfloat16

ROWS = 32
LAT = 40
WAVES = 32
COLS = 128
NWAVE = 1280
CELLS = LAT * WAVES
CHUNK = 256
CHUNKS = NWAVE // CHUNK
CHUNK_ORDER = (2, 4, 3, 1, 0)
STEP = 0.2


def far_partner(me, step):
    ring, inner = step // 4, step % 4
    size = (8 - ring) // 2
    shift = jnp.where(ring % 2 == 1, size, 8 - size)
    x, y, core = me // 16, (me // 2) % 8, me % 2
    return ((x + 1 - inner // 2) % 2) * 16 + ((y + shift) % 8) * 2 + (core + 1 - inner % 2) % 2


def kernel(
    state, legendre, gauss, mixing, surface, counts, source,
    new_state, new_surface,
    x_v, leg_v, gauss_s, mix_v, surf_v, count_s, source_v, partner_v,
    weight_v, send_v, recv_v, lat_v, acc_v, damp_v, filt_v, back_v, home_v, out_v,
    mask_v, block_v, u_v, edge_v, side_v, gap_v, surf_o,
    in_sem, out_sem, send_sem, recv_sem, back_send_sem, back_recv_sem, pair_sem, halo_send, halo_recv,
):
    comp = lax.axis_index("comp")
    me = lax.axis_index("row")
    col = lax.axis_index("col")
    n_col = lax.axis_size("col")
    air = comp == 0

    barrier = pltpu.get_barrier_semaphore()

    def greet(c, r, k):
        pl.semaphore_signal(barrier, inc=1, device_id=(c, r, k), device_id_type=MESH)

    loads = [
        pltpu.make_async_copy(src, dst, in_sem.at[i])
        for i, (src, dst) in enumerate(
            [(state, x_v), (gauss, gauss_s), (counts, count_s), (surface, surf_v), (source, source_v),
             (legendre, leg_v), (mixing, mix_v)]
        )
    ]
    load_state, load_gauss, load_counts, load_surface, load_source, load_legendre, load_mixing = loads

    greet(1 - comp, me, col)

    @pl.when(air)
    def _():
        def one(s, c):
            greet(0, far_partner(me, s), col)
            return c

        lax.fori_loop(0, ROWS - 1, one, 0)

    has = [me > 0, me < ROWS - 1, col > 0, col < n_col - 1]
    beside = [(1, me - 1, col), (1, me + 1, col), (1, me, col - 1), (1, me, col + 1)]

    @pl.when(jnp.logical_not(air))
    def _():
        for there, place in zip(has, beside):
            @pl.when(there)
            def _():
                greet(*place)

    for load in (load_state, load_gauss, load_counts, load_surface, load_source):
        load.start()

    pair_copy = pltpu.make_async_remote_copy(
        src_ref=surf_v, dst_ref=partner_v, send_sem=pair_sem.at[0], recv_sem=pair_sem.at[1],
        device_id=(1 - comp, me, col), device_id_type=MESH,
    )

    lane = lax.broadcasted_iota(jnp.int32, (1, COLS), 1)

    def surface_step(rate):
        pair_copy.wait_recv()
        for r in range(LAT):
            gap_v[r : r + 1, :] = (lane < count_s[r]).astype(F32)
        where_row = source_v[...] >> 7
        where_lane = source_v[...] & 127

        def one(r, total):
            row = jnp.broadcast_to(partner_v[pl.ds(r, 1), :], (LAT, COLS))
            got = jnp.take_along_axis(row, where_lane, axis=1)
            return jnp.where(where_row == r, got, total)

        pulled = lax.fori_loop(0, LAT, one, jnp.zeros((LAT, COLS), F32))
        gap = gap_v[...] * (pulled - surf_v[...])
        gap_v[...] = gap
        surf_o[...] = surf_v[...] + rate * gap

    @pl.when(air)
    def _():
        load_legendre.start()
        load_gauss.wait()
        for r in range(LAT):
            weight_v[r : r + 1, :] = jnp.full((1, COLS), gauss_s[r], F32)
        load_surface.wait()
        load_state.wait()
        pl.semaphore_wait(barrier, ROWS)
        weights = weight_v[...]

        def out_copy(p):
            return pltpu.make_async_remote_copy(
                src_ref=send_v.at[p], dst_ref=recv_v.at[me], send_sem=send_sem.at[p], recv_sem=recv_sem.at[me],
                device_id=(0, p, col), device_id_type=MESH,
            )

        def arrived(s):
            return pltpu.make_async_remote_copy(
                src_ref=send_v.at[s], dst_ref=recv_v.at[s], send_sem=send_sem.at[s], recv_sem=recv_sem.at[s],
                device_id=(0, me, col), device_id_type=MESH,
            )

        def send_one(s, c):
            p = far_partner(me, s)
            send_v[p] = (x_v[pl.ds(p, LAT, stride=WAVES), :] * weights).astype(BF16)
            out_copy(p).start()
            return c

        lax.fori_loop(0, ROWS - 1, send_one, 0)
        pair_copy.start()
        recv_v[me] = (x_v[pl.ds(me, LAT, stride=WAVES), :] * weights).astype(BF16)

        n = (lax.broadcasted_iota(jnp.int32, (1, NWAVE), 1) + me).astype(F32)
        ratio = n * (n + 1.0) / (1279.0 * 1280.0)
        damp_v[...] = 1.0 / (1.0 + 20.0 * ratio * ratio)
        load_legendre.wait()

        seen = set()
        for place, j in enumerate(CHUNK_ORDER):
            for s in range(CHUNK * j // LAT, (CHUNK * (j + 1) - 1) // LAT + 1):
                if s in seen:
                    continue
                seen.add(s)

                @pl.when(s != me)
                def _():
                    arrived(s).wait_recv()

                lat_v[s * LAT : (s + 1) * LAT, :] = recv_v[s].astype(F32)
            part = lat_v[j * CHUNK : (j + 1) * CHUNK, :].T.astype(BF16)
            product = jnp.dot(part, leg_v[j * CHUNK : (j + 1) * CHUNK, :], preferred_element_type=F32)
            if place == 0:
                acc_v[...] = product
            elif place < CHUNKS - 1:
                acc_v[...] += product
            else:
                filt_v[...] = (damp_v[...] * (acc_v[...] + product)).T.astype(BF16)

        def back_copy(p):
            return pltpu.make_async_remote_copy(
                src_ref=back_v.at[p], dst_ref=home_v.at[me], send_sem=back_send_sem.at[p],
                recv_sem=back_recv_sem.at[me], device_id=(0, p, col), device_id_type=MESH,
            )

        def back_arrived(s):
            return pltpu.make_async_remote_copy(
                src_ref=back_v.at[s], dst_ref=home_v.at[s], send_sem=back_send_sem.at[s],
                recv_sem=back_recv_sem.at[s], device_id=(0, me, col), device_id_type=MESH,
            )

        def synthesize(k, c):
            quarter = (me // 16 + 1 + k) % 2 * 2 + (me // 8 + 1 + k // 2) % 2
            block = jnp.dot(
                leg_v[pl.ds(pl.multiple_of(quarter * (8 * LAT), 8 * LAT), 8 * LAT), :], filt_v[...],
                preferred_element_type=F32,
            )
            for j in range(8):
                p = quarter * 8 + j
                back_v[p] = block[j * LAT : (j + 1) * LAT, :].astype(BF16)

                @pl.when(p != me)
                def _():
                    back_copy(p).start()

            return c

        lax.fori_loop(0, 4, synthesize, 0)
        home_v[me] = back_v[me]

        load_counts.wait()
        load_source.wait()
        surface_step(0.5)
        save = pltpu.make_async_copy(surf_o, new_surface, out_sem.at[4])
        save.start()

        for g in range(4):
            for m in range(g * 8, g * 8 + 8):
                @pl.when(m != me)
                def _():
                    back_arrived(m).wait_recv()

                out_v[pl.ds(m, LAT, stride=WAVES), :] = home_v[m].astype(F32)
        saves = pltpu.make_async_copy(out_v, new_state, out_sem.at[0])
        saves.start()

        def drain(s, c):
            p = far_partner(me, s)
            out_copy(p).wait_send()
            back_copy(p).wait_send()
            return c

        lax.fori_loop(0, ROWS - 1, drain, 0)
        pair_copy.wait_send()
        saves.wait()
        save.wait()

    @pl.when(jnp.logical_not(air))
    def _():
        load_mixing.start()
        load_surface.wait()
        total = sum(there.astype(jnp.int32) for there in has)
        load_counts.wait()
        for r in range(LAT):
            mask_v[r * WAVES : (r + 1) * WAVES, :] = jnp.broadcast_to((lane < count_s[r]).astype(F32), (WAVES, COLS))
        load_mixing.wait()
        pick = (lax.broadcasted_iota(jnp.int32, (CHUNK, WAVES), 0) & (WAVES - 1)) == lax.broadcasted_iota(
            jnp.int32, (CHUNK, WAVES), 1
        )
        pick = pick.astype(F32)
        tall = jnp.dot(pick, mix_v[...], precision=lax.Precision.HIGHEST, preferred_element_type=F32)
        wide = lax.dot_general(
            tall, pick, (((1,), (1,)), ((), ())), precision=lax.Precision.HIGHEST, preferred_element_type=F32
        )
        same = (lax.broadcasted_iota(jnp.int32, (CHUNK, CHUNK), 0) >> 5) == (
            lax.broadcasted_iota(jnp.int32, (CHUNK, CHUNK), 1) >> 5
        )
        block_v[...] = jnp.where(same, wide, 0.0)
        load_state.wait()
        for i in range(CHUNKS):
            part = slice(i * CHUNK, (i + 1) * CHUNK)
            mixed = jnp.dot(block_v[...], x_v[part, :], precision=lax.Precision.HIGHEST, preferred_element_type=F32)
            out_v[part, :] = x_v[part, :] + mask_v[part, :] * mixed
        pl.semaphore_wait(barrier, total + 1)
        pair_copy.start()

        def halo_copy(sweep, side):
            u = u_v.at[sweep]
            if side == 0:
                src, dst = u.at[pl.ds(WAVES, WAVES)], u.at[pl.ds(CELLS + WAVES, WAVES)]
            elif side == 1:
                src, dst = u.at[pl.ds(CELLS, WAVES)], u.at[pl.ds(0, WAVES)]
            else:
                src, dst = edge_v.at[sweep, side - 2], side_v.at[sweep, 3 - side]
            return pltpu.make_async_remote_copy(
                src_ref=src, dst_ref=dst, send_sem=halo_send.at[sweep, side], recv_sem=halo_recv.at[sweep, side ^ 1],
                device_id=beside[side], device_id_type=MESH,
            )

        def halo_arrived(sweep, side):
            u = u_v.at[sweep]
            if side == 0:
                dst = u.at[pl.ds(0, WAVES)]
            elif side == 1:
                dst = u.at[pl.ds(CELLS + WAVES, WAVES)]
            else:
                dst = side_v.at[sweep, side - 2]
            return pltpu.make_async_remote_copy(
                src_ref=dst, dst_ref=dst, send_sem=halo_send.at[sweep, side], recv_sem=halo_recv.at[sweep, side],
                device_id=(1, me, col), device_id_type=MESH,
            )

        for sweep in range(2):
            for i in range(CELLS // COLS):
                part = slice(i * COLS, (i + 1) * COLS)
                u = mask_v[part, :] * out_v[part, :]
                u_v[sweep, WAVES + i * COLS : WAVES + (i + 1) * COLS, :] = u
                flipped = u.T
                edge_v[sweep, 0, i : i + 1, :] = flipped[0:1, :]
                edge_v[sweep, 1, i : i + 1, :] = flipped[COLS - 1 : COLS, :]
            for side in range(4):
                @pl.when(has[side])
                def _():
                    halo_copy(sweep, side).start()

                @pl.when(jnp.logical_not(has[side]))
                def _():
                    if side == 0:
                        u_v[sweep, 0:WAVES, :] = jnp.zeros((WAVES, COLS), F32)
                    elif side == 1:
                        u_v[sweep, CELLS + WAVES : CELLS + 2 * WAVES, :] = jnp.zeros((WAVES, COLS), F32)
                    else:
                        side_v[sweep, side - 2] = jnp.zeros((16, COLS), F32)

            if sweep == 0:
                load_source.wait()
                surface_step(0.25)
                save = pltpu.make_async_copy(surf_o, new_surface, out_sem.at[4])
                save.start()
            for side in range(4):
                @pl.when(has[side])
                def _():
                    halo_arrived(sweep, side).wait_recv()

            west = side_v[sweep, 0].T
            east = side_v[sweep, 1].T
            for i in range(CELLS // COLS):
                part = slice(i * COLS, (i + 1) * COLS)
                low = i * COLS
                centre = u_v[sweep, low + WAVES : low + WAVES + COLS, :]
                left = jnp.where(lane == 0, west[:, i : i + 1], pltpu.roll(centre, 1, 1))
                right = jnp.where(lane == COLS - 1, east[:, i : i + 1], pltpu.roll(centre, COLS - 1, 1))
                above = u_v[sweep, low : low + COLS, :]
                below = u_v[sweep, low + 2 * WAVES : low + 2 * WAVES + COLS, :]
                laplace = above + below + left + right - 4.0 * centre
                out_v[part, :] = out_v[part, :] + STEP * mask_v[part, :] * laplace
        out_v[pl.ds(0, LAT, stride=WAVES), :] = out_v[pl.ds(0, LAT, stride=WAVES), :] + 0.3 * gap_v[...]
        saves = pltpu.make_async_copy(out_v, new_state, out_sem.at[0])
        saves.start()
        for sweep in range(2):
            for side in range(4):
                @pl.when(has[side])
                def _():
                    halo_copy(sweep, side).wait_send()
        load_gauss.wait()
        pair_copy.wait_send()
        saves.wait()
        save.wait()


def shards(model_state, legendre, gauss_weight, mixing, surface, sea_count, remap_source):
    anywhere = pl.BlockSpec(memory_space=pltpu.HBM)
    vmem = pltpu.VMEM
    dma = pltpu.SemaphoreType.DMA
    new_state, new_surface = pl.pallas_call(
        kernel,
        out_shape=(
            jax.ShapeDtypeStruct((CELLS, COLS), F32),
            jax.ShapeDtypeStruct((LAT, COLS), F32),
        ),
        in_specs=[anywhere] * 7,
        out_specs=(anywhere, anywhere),
        scratch_shapes=[
            vmem((CELLS, COLS), F32),
            vmem((NWAVE, NWAVE), BF16),
            pltpu.SMEM((LAT,), F32),
            vmem((WAVES, WAVES), F32),
            vmem((LAT, COLS), F32),
            pltpu.SMEM((LAT,), jnp.int32),
            vmem((LAT, COLS), jnp.int32),
            vmem((LAT, COLS), F32),
            vmem((LAT, COLS), F32),
            vmem((ROWS, LAT, COLS), BF16),
            vmem((ROWS, LAT, COLS), BF16),
            vmem((NWAVE, COLS), F32),
            vmem((COLS, NWAVE), F32),
            vmem((1, NWAVE), F32),
            vmem((NWAVE, COLS), BF16),
            vmem((ROWS, LAT, COLS), BF16),
            vmem((ROWS, LAT, COLS), BF16),
            vmem((CELLS, COLS), F32),
            vmem((CELLS, COLS), F32),
            vmem((CHUNK, CHUNK), F32),
            vmem((2, CELLS + 2 * WAVES, COLS), F32),
            vmem((2, 2, 16, COLS), F32),
            vmem((2, 2, 16, COLS), F32),
            vmem((LAT, COLS), F32),
            vmem((LAT, COLS), F32),
            dma((7,)), dma((5,)), dma((ROWS,)), dma((ROWS,)), dma((ROWS,)), dma((ROWS,)), dma((2,)),
            dma((2, 4)), dma((2, 4)),
        ],
        compiler_params=pltpu.CompilerParams(
            collective_id=0, has_side_effects=True, vmem_limit_bytes=63488 * 1024
        ),
        cost_estimate=pl.CostEstimate(flops=900_000_000, bytes_accessed=5_000_000, transcendentals=0),
    )(
        model_state.reshape(CELLS, COLS),
        legendre.reshape(NWAVE, NWAVE),
        gauss_weight,
        mixing,
        surface.reshape(LAT, COLS),
        sea_count.reshape(LAT),
        remap_source.reshape(LAT, COLS),
    )
    return new_state.reshape(1, LAT, WAVES, COLS), new_surface.reshape(1, LAT, COLS)


def solution(mesh):
    in_specs = (
        P("comp", "row", None, "col"),
        P("row", None, None),
        P("row"),
        P(),
        P("comp", "row", "col"),
        P("comp", "row", "col"),
        P("comp", "row", "col"),
    )
    out_specs = (P("comp", "row", None, "col"), P("comp", "row", "col"))
    return jax.shard_map(shards, mesh=mesh, in_specs=in_specs, out_specs=out_specs, check_vma=False)
```

```python
import functools

import jax
import jax.numpy as jnp
from jax import lax
from jax.experimental import pallas as pl
from jax.experimental.pallas import tpu as pltpu
from jax.sharding import PartitionSpec as P

MESH = pl.DeviceIdType.MESH
F32 = jnp.float32
BF16 = jnp.bfloat16

ROWS = 32
LAT = 40
WAVES = 32
COLS = 128
NWAVE = 1280
CELLS = LAT * WAVES
CHUNK = 256
CHUNKS = NWAVE // CHUNK
CHUNK_ORDER = (2, 4, 3, 1, 0)
STEP = 0.2


def far_partner(me, step):
    ring, inner = step // 4, step % 4
    size = (8 - ring) // 2
    shift = jnp.where(ring % 2 == 1, size, 8 - size)
    x, y, core = me // 16, (me // 2) % 8, me % 2
    return ((x + 1 - inner // 2) % 2) * 16 + ((y + shift) % 8) * 2 + (core + 1 - inner % 2) % 2


def kernel(
    state, legendre, gauss, mixing, surface, counts, source,
    new_state, new_surface,
    x_v, leg_v, gauss_s, mix_v, surf_v, count_s, source_v, partner_v,
    weight_v, send_v, recv_v, lat_v, acc_v, damp_v, filt_v, back_v, home_v,
    mask_v, block_v, u_v, edge_v, side_v, gap_v,
    in_sem, send_sem, recv_sem, back_send_sem, back_recv_sem, pair_sem, halo_send, halo_recv,
):
    comp = lax.axis_index("comp")
    me = lax.axis_index("row")
    col = lax.axis_index("col")
    n_col = lax.axis_size("col")
    air = comp == 0

    barrier = pltpu.get_barrier_semaphore()

    def greet(c, r, k):
        pl.semaphore_signal(barrier, inc=1, device_id=(c, r, k), device_id_type=MESH)

    loads = [
        pltpu.make_async_copy(src, dst, in_sem.at[i])
        for i, (src, dst) in enumerate(
            [(state, x_v), (gauss, gauss_s), (counts, count_s), (surface, surf_v), (source, source_v),
             (legendre, leg_v), (mixing, mix_v)]
        )
    ]
    load_state, load_gauss, load_counts, load_surface, load_source, load_legendre, load_mixing = loads

    greet(1 - comp, me, col)

    staged = col == 0
    follows = jnp.logical_and(staged, me > 0)

    @pl.when(jnp.logical_and(air, jnp.logical_not(jnp.logical_and(staged, me == 0))))
    def _():
        def one(s, c):
            p = far_partner(me, s)

            @pl.when(jnp.logical_not(jnp.logical_and(staged, p == 0)))
            def _():
                greet(0, p, col)

            return c

        lax.fori_loop(0, ROWS - 1, one, 0)

    has = [me > 0, me < ROWS - 1, col > 0, col < n_col - 1]
    beside = [(1, me - 1, col), (1, me + 1, col), (1, me, col - 1), (1, me, col + 1)]

    @pl.when(jnp.logical_not(air))
    def _():
        for there, place in zip(has, beside):
            @pl.when(there)
            def _():
                greet(*place)

    for load in (load_state, load_gauss, load_counts, load_surface, load_source):
        load.start()

    pair_copy = pltpu.make_async_remote_copy(
        src_ref=surf_v, dst_ref=partner_v, send_sem=pair_sem.at[0], recv_sem=pair_sem.at[1],
        device_id=(1 - comp, me, col), device_id_type=MESH,
    )

    lane = lax.broadcasted_iota(jnp.int32, (1, COLS), 1)

    def surface_step(rate):
        pair_copy.wait_recv()
        for r in range(LAT):
            gap_v[r : r + 1, :] = (lane < count_s[r]).astype(F32)
        where_row = source_v[...] >> 7
        where_lane = source_v[...] & 127

        def one(r, total):
            row = jnp.broadcast_to(partner_v[pl.ds(r, 1), :], (LAT, COLS))
            got = jnp.take_along_axis(row, where_lane, axis=1)
            return jnp.where(where_row == r, got, total)

        pulled = lax.fori_loop(0, LAT, one, jnp.zeros((LAT, COLS), F32))
        gap = gap_v[...] * (pulled - surf_v[...])
        gap_v[...] = gap
        new_surface[...] = surf_v[...] + rate * gap

    @pl.when(air)
    def _():
        load_legendre.start()
        load_gauss.wait()
        for r in range(LAT):
            weight_v[r : r + 1, :] = jnp.full((1, COLS), gauss_s[r], F32)
        load_surface.wait()
        load_state.wait()
        pl.semaphore_wait(barrier, jnp.where(follows, ROWS - 1, ROWS))

        @pl.when(follows)
        def _():
            greet(0, 0, col)

        @pl.when(jnp.logical_and(staged, me == 0))
        def _():
            def one(s, c):
                greet(0, far_partner(me, s), col)
                return c

            lax.fori_loop(0, ROWS - 1, one, 0)

        weights = weight_v[...]

        def out_copy(p):
            return pltpu.make_async_remote_copy(
                src_ref=send_v.at[p], dst_ref=recv_v.at[me], send_sem=send_sem.at[p], recv_sem=recv_sem.at[me],
                device_id=(0, p, col), device_id_type=MESH,
            )

        def arrived(s):
            return pltpu.make_async_remote_copy(
                src_ref=send_v.at[s], dst_ref=recv_v.at[s], send_sem=send_sem.at[s], recv_sem=recv_sem.at[s],
                device_id=(0, me, col), device_id_type=MESH,
            )

        def send_one(s, c):
            p = far_partner(me, s)
            send_v[p] = (x_v[pl.ds(p, LAT, stride=WAVES), :] * weights).astype(BF16)

            @pl.when(jnp.logical_not(jnp.logical_and(follows, p == 0)))
            def _():
                out_copy(p).start()

            return c

        lax.fori_loop(0, ROWS - 1, send_one, 0)
        pair_copy.start()
        recv_v[me] = (x_v[pl.ds(me, LAT, stride=WAVES), :] * weights).astype(BF16)

        n = (lax.broadcasted_iota(jnp.int32, (1, NWAVE), 1) + me).astype(F32)
        ratio = n * (n + 1.0) / (1279.0 * 1280.0)
        damp_v[...] = 1.0 / (1.0 + 20.0 * ratio * ratio)
        load_legendre.wait()

        seen = set()
        for place, j in enumerate(CHUNK_ORDER):
            if place == CHUNKS - 1:

                @pl.when(follows)
                def _():
                    pl.semaphore_wait(barrier, 1)
                    out_copy(0).start()

            for s in range(CHUNK * j // LAT, (CHUNK * (j + 1) - 1) // LAT + 1):
                if s in seen:
                    continue
                seen.add(s)

                @pl.when(s != me)
                def _():
                    arrived(s).wait_recv()

                lat_v[s * LAT : (s + 1) * LAT, :] = recv_v[s].astype(F32)
            part = lat_v[j * CHUNK : (j + 1) * CHUNK, :].T.astype(BF16)
            product = jnp.dot(part, leg_v[j * CHUNK : (j + 1) * CHUNK, :], preferred_element_type=F32)
            if place == 0:
                acc_v[...] = product
            elif place < CHUNKS - 1:
                acc_v[...] += product
            else:
                filt_v[...] = (damp_v[...] * (acc_v[...] + product)).T.astype(BF16)

        def back_copy(p):
            return pltpu.make_async_remote_copy(
                src_ref=back_v.at[p], dst_ref=home_v.at[me], send_sem=back_send_sem.at[p],
                recv_sem=back_recv_sem.at[me], device_id=(0, p, col), device_id_type=MESH,
            )

        def back_arrived(s):
            return pltpu.make_async_remote_copy(
                src_ref=back_v.at[s], dst_ref=home_v.at[s], send_sem=back_send_sem.at[s],
                recv_sem=back_recv_sem.at[s], device_id=(0, me, col), device_id_type=MESH,
            )

        def synthesize(k, c):
            quarter = (me // 16 + 1 + k) % 2 * 2 + (me // 8 + 1 + k // 2) % 2
            block = jnp.dot(
                leg_v[pl.ds(pl.multiple_of(quarter * (8 * LAT), 8 * LAT), 8 * LAT), :], filt_v[...],
                preferred_element_type=F32,
            )
            for j in range(8):
                p = quarter * 8 + j
                back_v[p] = block[j * LAT : (j + 1) * LAT, :].astype(BF16)

                @pl.when(p != me)
                def _():
                    back_copy(p).start()

            return c

        lax.fori_loop(0, 4, synthesize, 0)
        home_v[me] = back_v[me]

        load_counts.wait()
        load_source.wait()
        surface_step(0.5)

        def take_home(m):
            @pl.when(m != me)
            def _():
                back_arrived(m).wait_recv()

            new_state[pl.ds(m, LAT, stride=WAVES), :] = home_v[m].astype(F32)

        def near(s, c):
            m = far_partner(me, ROWS - 1 - s)

            @pl.when(m != 0)
            def _():
                take_home(m)

            return c

        lax.fori_loop(0, ROWS, near, 0)
        take_home(0)

        def drain(s, c):
            p = far_partner(me, s)
            out_copy(p).wait_send()
            back_copy(p).wait_send()
            return c

        lax.fori_loop(0, ROWS - 1, drain, 0)
        pair_copy.wait_send()

    @pl.when(jnp.logical_not(air))
    def _():
        load_mixing.start()
        load_surface.wait()
        total = sum(there.astype(jnp.int32) for there in has)
        load_counts.wait()
        for r in range(LAT):
            mask_v[r * WAVES : (r + 1) * WAVES, :] = jnp.broadcast_to((lane < count_s[r]).astype(F32), (WAVES, COLS))
        load_mixing.wait()
        pick = (lax.broadcasted_iota(jnp.int32, (CHUNK, WAVES), 0) & (WAVES - 1)) == lax.broadcasted_iota(
            jnp.int32, (CHUNK, WAVES), 1
        )
        pick = pick.astype(F32)
        tall = jnp.dot(pick, mix_v[...], precision=lax.Precision.HIGHEST, preferred_element_type=F32)
        wide = lax.dot_general(
            tall, pick, (((1,), (1,)), ((), ())), precision=lax.Precision.HIGHEST, preferred_element_type=F32
        )
        same = (lax.broadcasted_iota(jnp.int32, (CHUNK, CHUNK), 0) >> 5) == (
            lax.broadcasted_iota(jnp.int32, (CHUNK, CHUNK), 1) >> 5
        )
        block_v[...] = jnp.where(same, wide, 0.0)
        load_state.wait()
        for i in range(CHUNKS):
            part = slice(i * CHUNK, (i + 1) * CHUNK)
            mixed = jnp.dot(block_v[...], x_v[part, :], precision=lax.Precision.HIGHEST, preferred_element_type=F32)
            new_state[part, :] = x_v[part, :] + mask_v[part, :] * mixed
        pl.semaphore_wait(barrier, total + 1)
        pair_copy.start()

        def halo_copy(sweep, side):
            u = u_v.at[sweep]
            if side == 0:
                src, dst = u.at[pl.ds(WAVES, WAVES)], u.at[pl.ds(CELLS + WAVES, WAVES)]
            elif side == 1:
                src, dst = u.at[pl.ds(CELLS, WAVES)], u.at[pl.ds(0, WAVES)]
            else:
                src, dst = edge_v.at[sweep, side - 2], side_v.at[sweep, 3 - side]
            return pltpu.make_async_remote_copy(
                src_ref=src, dst_ref=dst, send_sem=halo_send.at[sweep, side], recv_sem=halo_recv.at[sweep, side ^ 1],
                device_id=beside[side], device_id_type=MESH,
            )

        def halo_arrived(sweep, side):
            u = u_v.at[sweep]
            if side == 0:
                dst = u.at[pl.ds(0, WAVES)]
            elif side == 1:
                dst = u.at[pl.ds(CELLS + WAVES, WAVES)]
            else:
                dst = side_v.at[sweep, side - 2]
            return pltpu.make_async_remote_copy(
                src_ref=dst, dst_ref=dst, send_sem=halo_send.at[sweep, side], recv_sem=halo_recv.at[sweep, side],
                device_id=(1, me, col), device_id_type=MESH,
            )

        for sweep in range(2):
            for i in range(CELLS // COLS):
                part = slice(i * COLS, (i + 1) * COLS)
                u = mask_v[part, :] * new_state[part, :]
                u_v[sweep, WAVES + i * COLS : WAVES + (i + 1) * COLS, :] = u
                flipped = u.T
                edge_v[sweep, 0, i : i + 1, :] = flipped[0:1, :]
                edge_v[sweep, 1, i : i + 1, :] = flipped[COLS - 1 : COLS, :]
            for side in range(4):
                @pl.when(has[side])
                def _():
                    halo_copy(sweep, side).start()

                @pl.when(jnp.logical_not(has[side]))
                def _():
                    if side == 0:
                        u_v[sweep, 0:WAVES, :] = jnp.zeros((WAVES, COLS), F32)
                    elif side == 1:
                        u_v[sweep, CELLS + WAVES : CELLS + 2 * WAVES, :] = jnp.zeros((WAVES, COLS), F32)
                    else:
                        side_v[sweep, side - 2] = jnp.zeros((16, COLS), F32)

            if sweep == 0:
                load_source.wait()
                surface_step(0.25)
            for side in range(4):
                @pl.when(has[side])
                def _():
                    halo_arrived(sweep, side).wait_recv()

            west = side_v[sweep, 0].T
            east = side_v[sweep, 1].T
            for i in range(CELLS // COLS):
                part = slice(i * COLS, (i + 1) * COLS)
                low = i * COLS
                centre = u_v[sweep, low + WAVES : low + WAVES + COLS, :]
                left = jnp.where(lane == 0, west[:, i : i + 1], pltpu.roll(centre, 1, 1))
                right = jnp.where(lane == COLS - 1, east[:, i : i + 1], pltpu.roll(centre, COLS - 1, 1))
                above = u_v[sweep, low : low + COLS, :]
                below = u_v[sweep, low + 2 * WAVES : low + 2 * WAVES + COLS, :]
                laplace = above + below + left + right - 4.0 * centre
                new_state[part, :] = new_state[part, :] + STEP * mask_v[part, :] * laplace
        new_state[pl.ds(0, LAT, stride=WAVES), :] = new_state[pl.ds(0, LAT, stride=WAVES), :] + 0.3 * gap_v[...]
        for sweep in range(2):
            for side in range(4):
                @pl.when(has[side])
                def _():
                    halo_copy(sweep, side).wait_send()
        load_gauss.wait()
        pair_copy.wait_send()


def shards(model_state, legendre, gauss_weight, mixing, surface, sea_count, remap_source):
    anywhere = pl.BlockSpec(memory_space=pl.ANY)
    vmem = pltpu.VMEM
    dma = pltpu.SemaphoreType.DMA
    new_state, new_surface = pl.pallas_call(
        kernel,
        out_shape=(
            pltpu.VMEM((CELLS, COLS), F32),
            pltpu.VMEM((LAT, COLS), F32),
        ),
        in_specs=[anywhere] * 7,
        out_specs=(pl.BlockSpec(memory_space=vmem),) * 2,
        scratch_shapes=[
            vmem((CELLS, COLS), F32),
            vmem((NWAVE, NWAVE), BF16),
            pltpu.SMEM((LAT,), F32),
            vmem((WAVES, WAVES), F32),
            vmem((LAT, COLS), F32),
            pltpu.SMEM((LAT,), jnp.int32),
            vmem((LAT, COLS), jnp.int32),
            vmem((LAT, COLS), F32),
            vmem((LAT, COLS), F32),
            vmem((ROWS, LAT, COLS), BF16),
            vmem((ROWS, LAT, COLS), BF16),
            vmem((NWAVE, COLS), F32),
            vmem((COLS, NWAVE), F32),
            vmem((1, NWAVE), F32),
            vmem((NWAVE, COLS), BF16),
            vmem((ROWS, LAT, COLS), BF16),
            vmem((ROWS, LAT, COLS), BF16),
            vmem((CELLS, COLS), F32),
            vmem((CHUNK, CHUNK), F32),
            vmem((2, CELLS + 2 * WAVES, COLS), F32),
            vmem((2, 2, 16, COLS), F32),
            vmem((2, 2, 16, COLS), F32),
            vmem((LAT, COLS), F32),
            dma((7,)), dma((ROWS,)), dma((ROWS,)), dma((ROWS,)), dma((ROWS,)), dma((2,)),
            dma((2, 4)), dma((2, 4)),
        ],
        compiler_params=pltpu.CompilerParams(
            collective_id=0, has_side_effects=True, vmem_limit_bytes=48 * 1024 * 1024
        ),
        cost_estimate=pl.CostEstimate(flops=900_000_000, bytes_accessed=5_000_000, transcendentals=0),
    )(
        *(
            pltpu.with_memory_space_constraint(operand, pltpu.HBM)
            for operand in (
                model_state.reshape(CELLS, COLS),
                legendre.reshape(NWAVE, NWAVE),
                gauss_weight,
                mixing,
                surface.reshape(LAT, COLS),
                sea_count.reshape(LAT),
                remap_source.reshape(LAT, COLS),
            )
        )
    )
    return new_state.reshape(1, LAT, WAVES, COLS), new_surface.reshape(1, LAT, COLS)


def solution(mesh):
    in_specs = (
        P("comp", "row", None, "col"),
        P("row", None, None),
        P("row"),
        P(),
        P("comp", "row", "col"),
        P("comp", "row", "col"),
        P("comp", "row", "col"),
    )
    out_specs = (P("comp", "row", None, "col"), P("comp", "row", "col"))
    return jax.shard_map(shards, mesh=mesh, in_specs=in_specs, out_specs=out_specs, check_vma=False)
```

```python
import functools

import jax
import jax.numpy as jnp
from jax import lax
from jax.experimental import pallas as pl
from jax.experimental.pallas import tpu as pltpu
from jax.sharding import PartitionSpec as P

MESH = pl.DeviceIdType.MESH
F32 = jnp.float32
BF16 = jnp.bfloat16

ROWS = 32
LAT = 40
WAVES = 32
COLS = 128
NWAVE = 1280
CELLS = LAT * WAVES
CHUNK = 256
CHUNKS = NWAVE // CHUNK
CHUNK_ORDER = (2, 4, 3, 1, 0)
STEP = 0.2


def far_partner(me, step):
    ring, inner = step // 4, step % 4
    shift = (8 - ring) // 2 if ring % 2 else 8 - (8 - ring) // 2
    flip = (1 - inner // 2) * 16 + (1 - inner % 2)
    return ((me & 17) ^ flip) + ((me + 2 * shift) & 14)


def kernel(
    state, legendre, gauss, mixing, surface, counts, source,
    new_state, new_surface,
    x_v, leg_v, gauss_s, mix_v, surf_v, count_s, source_v, partner_v,
    weight_v, send_v, recv_v, lat_v, acc_v, damp_v, filt_v, back_v, home_v,
    mask_v, block_v, u_v, edge_v, side_v, gap_v,
    in_sem, send_sem, recv_sem, back_send_sem, back_recv_sem, pair_sem, halo_send, halo_recv,
):
    comp = lax.axis_index("comp")
    me = lax.axis_index("row")
    col = lax.axis_index("col")
    n_col = lax.axis_size("col")
    air = comp == 0

    barrier = pltpu.get_barrier_semaphore()

    def greet(c, r, k):
        pl.semaphore_signal(barrier, inc=1, device_id=(c, r, k), device_id_type=MESH)

    loads = [
        pltpu.make_async_copy(src, dst, in_sem.at[i])
        for i, (src, dst) in enumerate(
            [(state, x_v), (gauss, gauss_s), (counts, count_s), (surface, surf_v), (source, source_v),
             (legendre, leg_v), (mixing, mix_v)]
        )
    ]
    load_state, load_gauss, load_counts, load_surface, load_source, load_legendre, load_mixing = loads

    staged = col == 0
    late = jnp.logical_and(jnp.logical_and(staged, me == 0), air)
    helper = jnp.logical_and(jnp.logical_and(staged, me == 0), jnp.logical_not(air))
    early = jnp.logical_or(jnp.logical_and(jnp.logical_and(staged, me > 0), air), helper)
    works = jnp.logical_or(jnp.logical_and(air, jnp.logical_not(late)), helper)

    def wave_comp(p):
        return jnp.where(jnp.logical_and(staged, p == 0), 1, 0)

    @pl.when(jnp.logical_not(jnp.logical_or(late, helper)))
    def _():
        greet(1 - comp, me, col)

    @pl.when(works)
    def _():
        for s in range(ROWS - 1):
            p = far_partner(me, s)
            greet(wave_comp(p), p, col)

    has = [me > 0, me < ROWS - 1, col > 0, col < n_col - 1]
    beside = [(1, me - 1, col), (1, me + 1, col), (1, me, col - 1), (1, me, col + 1)]

    @pl.when(jnp.logical_not(air))
    def _():
        for there, place in zip(has, beside):
            @pl.when(there)
            def _():
                greet(*place)

    for load in (load_state, load_gauss, load_counts, load_surface, load_source):
        load.start()

    @pl.when(works)
    def _():
        load_legendre.start()

    pair_copy = pltpu.make_async_remote_copy(
        src_ref=surf_v, dst_ref=partner_v, send_sem=pair_sem.at[0], recv_sem=pair_sem.at[1],
        device_id=(1 - comp, me, col), device_id_type=MESH,
    )

    lane = lax.broadcasted_iota(jnp.int32, (1, COLS), 1)

    def surface_step(rate):
        pair_copy.wait_recv()
        for r in range(LAT):
            gap_v[r : r + 1, :] = (lane < count_s[r]).astype(F32)
        where_row = source_v[...] >> 7
        where_lane = source_v[...] & 127

        def one(r, total):
            row = jnp.broadcast_to(partner_v[pl.ds(r, 1), :], (LAT, COLS))
            got = jnp.take_along_axis(row, where_lane, axis=1)
            return jnp.where(where_row == r, got, total)

        pulled = lax.fori_loop(0, LAT, one, jnp.zeros((LAT, COLS), F32))
        gap = gap_v[...] * (pulled - surf_v[...])
        gap_v[...] = gap
        new_surface[...] = surf_v[...] + rate * gap

    def out_copy(p):
        return pltpu.make_async_remote_copy(
            src_ref=send_v.at[p], dst_ref=recv_v.at[me], send_sem=send_sem.at[p], recv_sem=recv_sem.at[me],
            device_id=(wave_comp(p), p, col), device_id_type=MESH,
        )

    def arrived(s):
        return pltpu.make_async_remote_copy(
            src_ref=send_v.at[s], dst_ref=recv_v.at[s], send_sem=send_sem.at[s], recv_sem=recv_sem.at[s],
            device_id=(0, s, col), device_id_type=MESH,
        )

    def back_copy(p):
        return pltpu.make_async_remote_copy(
            src_ref=back_v.at[p], dst_ref=home_v.at[me], send_sem=back_send_sem.at[p],
            recv_sem=back_recv_sem.at[me], device_id=(0, p, col), device_id_type=MESH,
        )

    def back_arrived(s):
        return pltpu.make_async_remote_copy(
            src_ref=back_v.at[s], dst_ref=home_v.at[s], send_sem=back_send_sem.at[s],
            recv_sem=back_recv_sem.at[s], device_id=(0, s, col), device_id_type=MESH,
        )

    def take_home(m):
        back_arrived(m).wait_recv()
        new_state[pl.ds(m, LAT, stride=WAVES), :] = home_v[m].astype(F32)

    def elsewhere(r):
        return jnp.logical_not(jnp.logical_and(works, jnp.logical_and(air, r == me)))

    @pl.when(air)
    def _():
        load_gauss.wait()
        for r in range(LAT):
            weight_v[r : r + 1, :] = jnp.full((1, COLS), gauss_s[r], F32)
        load_surface.wait()
        load_state.wait()
        pl.semaphore_wait(barrier, ROWS)

        @pl.when(early)
        def _():
            greet(0, 0, col)

        weights = weight_v[...]

        for s in range(ROWS - 1):
            p = far_partner(me, s)
            send_v[p] = (x_v[pl.ds(p, LAT, stride=WAVES), :] * weights).astype(BF16)
            out_copy(p).start()

        own = (x_v[pl.ds(me, LAT, stride=WAVES), :] * weights).astype(BF16)

        @pl.when(late)
        def _():
            send_v[me] = own
            out_copy(me).start()
            greet(1, me, col)

            for s in range(ROWS - 1):
                greet(0, far_partner(me, s), col)

        @pl.when(jnp.logical_not(late))
        def _():
            recv_v[me] = own

        pair_copy.start()

    @pl.when(jnp.logical_not(air))
    def _():
        load_mixing.start()
        load_surface.wait()
        total = sum(there.astype(jnp.int32) for there in has)
        load_counts.wait()
        for r in range(LAT):
            mask_v[r * WAVES : (r + 1) * WAVES, :] = jnp.broadcast_to((lane < count_s[r]).astype(F32), (WAVES, COLS))
        load_mixing.wait()
        pick = (lax.broadcasted_iota(jnp.int32, (CHUNK, WAVES), 0) & (WAVES - 1)) == lax.broadcasted_iota(
            jnp.int32, (CHUNK, WAVES), 1
        )
        pick = pick.astype(F32)
        tall = jnp.dot(pick, mix_v[...], precision=lax.Precision.HIGHEST, preferred_element_type=F32)
        wide = lax.dot_general(
            tall, pick, (((1,), (1,)), ((), ())), precision=lax.Precision.HIGHEST, preferred_element_type=F32
        )
        same = (lax.broadcasted_iota(jnp.int32, (CHUNK, CHUNK), 0) >> 5) == (
            lax.broadcasted_iota(jnp.int32, (CHUNK, CHUNK), 1) >> 5
        )
        block_v[...] = jnp.where(same, wide, 0.0)
        load_state.wait()
        for i in range(CHUNKS):
            part = slice(i * CHUNK, (i + 1) * CHUNK)
            mixed = jnp.dot(block_v[...], x_v[part, :], precision=lax.Precision.HIGHEST, preferred_element_type=F32)
            new_state[part, :] = x_v[part, :] + mask_v[part, :] * mixed
        pl.semaphore_wait(barrier, total + jnp.where(helper, ROWS - 1, 1))

        @pl.when(helper)
        def _():
            greet(0, 0, col)

        @pl.when(jnp.logical_not(helper))
        def _():
            pair_copy.start()

        def halo_copy(sweep, side):
            u = u_v.at[sweep]
            if side == 0:
                src, dst = u.at[pl.ds(WAVES, WAVES)], u.at[pl.ds(CELLS + WAVES, WAVES)]
            elif side == 1:
                src, dst = u.at[pl.ds(CELLS, WAVES)], u.at[pl.ds(0, WAVES)]
            else:
                src, dst = edge_v.at[sweep, side - 2], side_v.at[sweep, 3 - side]
            return pltpu.make_async_remote_copy(
                src_ref=src, dst_ref=dst, send_sem=halo_send.at[sweep, side], recv_sem=halo_recv.at[sweep, side ^ 1],
                device_id=beside[side], device_id_type=MESH,
            )

        def halo_arrived(sweep, side):
            u = u_v.at[sweep]
            if side == 0:
                dst = u.at[pl.ds(0, WAVES)]
            elif side == 1:
                dst = u.at[pl.ds(CELLS + WAVES, WAVES)]
            else:
                dst = side_v.at[sweep, side - 2]
            return pltpu.make_async_remote_copy(
                src_ref=dst, dst_ref=dst, send_sem=halo_send.at[sweep, side], recv_sem=halo_recv.at[sweep, side],
                device_id=(1, me, col), device_id_type=MESH,
            )

        for sweep in range(2):
            for i in range(CELLS // COLS):
                part = slice(i * COLS, (i + 1) * COLS)
                u = mask_v[part, :] * new_state[part, :]
                u_v[sweep, WAVES + i * COLS : WAVES + (i + 1) * COLS, :] = u
                flipped = u.T
                edge_v[sweep, 0, i : i + 1, :] = flipped[0:1, :]
                edge_v[sweep, 1, i : i + 1, :] = flipped[COLS - 1 : COLS, :]
            for side in range(4):
                @pl.when(has[side])
                def _():
                    halo_copy(sweep, side).start()

                @pl.when(jnp.logical_not(has[side]))
                def _():
                    if side == 0:
                        u_v[sweep, 0:WAVES, :] = jnp.zeros((WAVES, COLS), F32)
                    elif side == 1:
                        u_v[sweep, CELLS + WAVES : CELLS + 2 * WAVES, :] = jnp.zeros((WAVES, COLS), F32)
                    else:
                        side_v[sweep, side - 2] = jnp.zeros((16, COLS), F32)

            for side in range(4):
                @pl.when(has[side])
                def _():
                    halo_arrived(sweep, side).wait_recv()

            west = side_v[sweep, 0].T
            east = side_v[sweep, 1].T
            for i in range(CELLS // COLS):
                part = slice(i * COLS, (i + 1) * COLS)
                low = i * COLS
                centre = u_v[sweep, low + WAVES : low + WAVES + COLS, :]
                left = jnp.where(lane == 0, west[:, i : i + 1], pltpu.roll(centre, 1, 1))
                right = jnp.where(lane == COLS - 1, east[:, i : i + 1], pltpu.roll(centre, COLS - 1, 1))
                above = u_v[sweep, low : low + COLS, :]
                below = u_v[sweep, low + 2 * WAVES : low + 2 * WAVES + COLS, :]
                laplace = above + below + left + right - 4.0 * centre
                new_state[part, :] = new_state[part, :] + STEP * mask_v[part, :] * laplace
        for sweep in range(2):
            for side in range(4):
                @pl.when(has[side])
                def _():
                    halo_copy(sweep, side).wait_send()

    @pl.when(works)
    def _():
        n = (lax.broadcasted_iota(jnp.int32, (1, NWAVE), 1) + me).astype(F32)
        ratio = n * (n + 1.0) / (1279.0 * 1280.0)
        damp_v[...] = 1.0 / (1.0 + 20.0 * ratio * ratio)
        load_legendre.wait()

        seen = set()
        for place, j in enumerate(CHUNK_ORDER):
            if place == CHUNKS - 1:

                @pl.when(early)
                def _():
                    pl.semaphore_wait(barrier, 1)

                @pl.when(helper)
                def _():
                    pair_copy.start()

            for s in range(CHUNK * j // LAT, (CHUNK * (j + 1) - 1) // LAT + 1):
                if s in seen:
                    continue
                seen.add(s)

                @pl.when(elsewhere(s))
                def _():
                    arrived(s).wait_recv()

                lat_v[s * LAT : (s + 1) * LAT, :] = recv_v[s].astype(F32)
            part = lat_v[j * CHUNK : (j + 1) * CHUNK, :].T.astype(BF16)
            product = jnp.dot(part, leg_v[j * CHUNK : (j + 1) * CHUNK, :], preferred_element_type=F32)
            if place == 0:
                acc_v[...] = product
            elif place < CHUNKS - 1:
                acc_v[...] += product
            else:
                filt_v[...] = (damp_v[...] * (acc_v[...] + product)).T.astype(BF16)

        for k in range(4):
            quarter = (me >> 3) ^ (3, 2, 1, 0)[k]
            block = jnp.dot(
                leg_v[pl.ds(pl.multiple_of(quarter * (8 * LAT), 8 * LAT), 8 * LAT), :], filt_v[...],
                preferred_element_type=F32,
            )
            for j in range(8):
                p = quarter * 8 + j
                back_v[p] = block[j * LAT : (j + 1) * LAT, :].astype(BF16)
                if k < 3:
                    back_copy(p).start()
                else:

                    @pl.when(elsewhere(p))
                    def _():
                        back_copy(p).start()

        @pl.when(air)
        def _():
            home_v[me] = back_v[me]

    @pl.when(air)
    def _():
        load_counts.wait()
        load_source.wait()
        surface_step(0.5)

        for s in range(ROWS - 1):
            out_copy(far_partner(me, s)).wait_send()

        @pl.when(late)
        def _():
            out_copy(me).wait_send()
            take_home(me)

        @pl.when(jnp.logical_not(late))
        def _():
            new_state[pl.ds(me, LAT, stride=WAVES), :] = home_v[me].astype(F32)

        pair_copy.wait_send()
        for s in range(ROWS - 2, 8, -1):
            take_home(far_partner(me, s))

    @pl.when(works)
    def _():
        for s in range(ROWS - 1):
            back_copy(far_partner(me, s)).wait_send()

        @pl.when(helper)
        def _():
            back_copy(me).wait_send()

    @pl.when(air)
    def _():
        for s in range(8, -1, -1):
            take_home(far_partner(me, s))

    @pl.when(jnp.logical_not(air))
    def _():
        load_source.wait()
        surface_step(0.25)
        new_state[pl.ds(0, LAT, stride=WAVES), :] = new_state[pl.ds(0, LAT, stride=WAVES), :] + 0.3 * gap_v[...]
        load_gauss.wait()
        pair_copy.wait_send()


def shards(model_state, legendre, gauss_weight, mixing, surface, sea_count, remap_source):
    anywhere = pl.BlockSpec(memory_space=pl.ANY)
    vmem = pltpu.VMEM
    dma = pltpu.SemaphoreType.DMA
    new_state, new_surface = pl.pallas_call(
        kernel,
        out_shape=(
            pltpu.VMEM((CELLS, COLS), F32),
            pltpu.VMEM((LAT, COLS), F32),
        ),
        in_specs=[anywhere] * 7,
        out_specs=(pl.BlockSpec(memory_space=vmem),) * 2,
        scratch_shapes=[
            vmem((CELLS, COLS), F32),
            vmem((NWAVE, NWAVE), BF16),
            pltpu.SMEM((LAT,), F32),
            vmem((WAVES, WAVES), F32),
            vmem((LAT, COLS), F32),
            pltpu.SMEM((LAT,), jnp.int32),
            vmem((LAT, COLS), jnp.int32),
            vmem((LAT, COLS), F32),
            vmem((LAT, COLS), F32),
            vmem((ROWS, LAT, COLS), BF16),
            vmem((ROWS, LAT, COLS), BF16),
            vmem((NWAVE, COLS), F32),
            vmem((COLS, NWAVE), F32),
            vmem((1, NWAVE), F32),
            vmem((NWAVE, COLS), BF16),
            vmem((ROWS, LAT, COLS), BF16),
            vmem((ROWS, LAT, COLS), BF16),
            vmem((CELLS, COLS), F32),
            vmem((CHUNK, CHUNK), F32),
            vmem((2, CELLS + 2 * WAVES, COLS), F32),
            vmem((2, 2, 16, COLS), F32),
            vmem((2, 2, 16, COLS), F32),
            vmem((LAT, COLS), F32),
            dma((7,)), dma((ROWS,)), dma((ROWS,)), dma((ROWS,)), dma((ROWS,)), dma((2,)),
            dma((2, 4)), dma((2, 4)),
        ],
        compiler_params=pltpu.CompilerParams(
            collective_id=0, has_side_effects=True, vmem_limit_bytes=48 * 1024 * 1024
        ),
        cost_estimate=pl.CostEstimate(flops=900_000_000, bytes_accessed=5_000_000, transcendentals=0),
    )(
        *(
            pltpu.with_memory_space_constraint(operand, pltpu.HBM)
            for operand in (
                model_state.reshape(CELLS, COLS),
                legendre.reshape(NWAVE, NWAVE),
                gauss_weight,
                mixing,
                surface.reshape(LAT, COLS),
                sea_count.reshape(LAT),
                remap_source.reshape(LAT, COLS),
            )
        )
    )
    return new_state.reshape(1, LAT, WAVES, COLS), new_surface.reshape(1, LAT, COLS)


def solution(mesh):
    in_specs = (
        P("comp", "row", None, "col"),
        P("row", None, None),
        P("row"),
        P(),
        P("comp", "row", "col"),
        P("comp", "row", "col"),
        P("comp", "row", "col"),
    )
    out_specs = (P("comp", "row", None, "col"), P("comp", "row", "col"))
    return jax.shard_map(shards, mesh=mesh, in_specs=in_specs, out_specs=out_specs, check_vma=False)
```

```python
import functools

import jax
import jax.numpy as jnp
from jax import lax
from jax.experimental import pallas as pl
from jax.experimental.pallas import tpu as pltpu
from jax.sharding import PartitionSpec as P

MESH = pl.DeviceIdType.MESH
F32 = jnp.float32
BF16 = jnp.bfloat16

ROWS = 32
LAT = 40
WAVES = 32
COLS = 128
NWAVE = 1280
CELLS = LAT * WAVES
CHUNK = 256
CHUNKS = NWAVE // CHUNK
CHUNK_ORDER = (2, 4, 3, 1, 0)
STEP = 0.2
SAVES = 4


def far_partner(me, step):
    ring, inner = step // 4, step % 4
    shift = (8 - ring) // 2 if ring % 2 else 8 - (8 - ring) // 2
    flip = (1 - inner // 2) * 16 + (1 - inner % 2)
    return ((me & 17) ^ flip) + ((me + 2 * shift) & 14)


def kernel(
    state, legendre, gauss, mixing, surface, counts, source,
    new_state, new_surface,
    x_v, leg_v, gauss_s, mix_v, surf_v, count_s, source_v, partner_v,
    weight_v, send_v, recv_v, lat_v, acc_v, damp_v, filt_v, back_v, home_v,
    mask_v, block_v, u_v, edge_v, side_v, gap_v,
    in_sem, send_sem, recv_sem, back_send_sem, back_recv_sem, pair_sem, halo_send, halo_recv,
):
    comp = lax.axis_index("comp")
    me = lax.axis_index("row")
    col = lax.axis_index("col")
    n_col = lax.axis_size("col")
    air = comp == 0

    barrier = pltpu.get_barrier_semaphore()

    def greet(c, r, k):
        pl.semaphore_signal(barrier, inc=1, device_id=(c, r, k), device_id_type=MESH)

    loads = [
        pltpu.make_async_copy(src, dst, in_sem.at[i])
        for i, (src, dst) in enumerate(
            [(state, x_v), (gauss, gauss_s), (counts, count_s), (surface, surf_v), (source, source_v),
             (legendre, leg_v), (mixing, mix_v)]
        )
    ]
    load_state, load_gauss, load_counts, load_surface, load_source, load_legendre, load_mixing = loads

    staged = col == 0
    late = jnp.logical_and(jnp.logical_and(staged, me == 0), air)
    helper = jnp.logical_and(jnp.logical_and(staged, me == 0), jnp.logical_not(air))
    early = jnp.logical_or(jnp.logical_and(jnp.logical_and(staged, me > 0), air), helper)
    works = jnp.logical_or(jnp.logical_and(air, jnp.logical_not(late)), helper)

    def wave_comp(p):
        return jnp.where(jnp.logical_and(staged, p == 0), 1, 0)

    @pl.when(jnp.logical_not(jnp.logical_or(late, helper)))
    def _():
        greet(1 - comp, me, col)

    @pl.when(works)
    def _():
        for s in range(ROWS - 1):
            p = far_partner(me, s)
            greet(wave_comp(p), p, col)

    has = [me > 0, me < ROWS - 1, col > 0, col < n_col - 1]
    beside = [(1, me - 1, col), (1, me + 1, col), (1, me, col - 1), (1, me, col + 1)]

    @pl.when(jnp.logical_not(air))
    def _():
        for there, place in zip(has, beside):
            @pl.when(there)
            def _():
                greet(*place)

    for load in (load_state, load_gauss, load_counts, load_surface, load_source):
        load.start()

    @pl.when(works)
    def _():
        load_legendre.start()

    pair_copy = pltpu.make_async_remote_copy(
        src_ref=surf_v, dst_ref=partner_v, send_sem=pair_sem.at[0], recv_sem=pair_sem.at[1],
        device_id=(1 - comp, me, col), device_id_type=MESH,
    )

    lane = lax.broadcasted_iota(jnp.int32, (1, COLS), 1)

    def surface_step(rate):
        pair_copy.wait_recv()
        for r in range(LAT):
            gap_v[r : r + 1, :] = (lane < count_s[r]).astype(F32)
        where_row = source_v[...] >> 7
        where_lane = source_v[...] & 127

        def one(r, total):
            row = jnp.broadcast_to(partner_v[pl.ds(r, 1), :], (LAT, COLS))
            got = jnp.take_along_axis(row, where_lane, axis=1)
            return jnp.where(where_row == r, got, total)

        pulled = lax.fori_loop(0, LAT, one, jnp.zeros((LAT, COLS), F32))
        gap = gap_v[...] * (pulled - surf_v[...])
        gap_v[...] = gap
        new_surface[...] = surf_v[...] + rate * gap

    def out_copy(p):
        return pltpu.make_async_remote_copy(
            src_ref=send_v.at[p], dst_ref=recv_v.at[me], send_sem=send_sem.at[p], recv_sem=recv_sem.at[me],
            device_id=(wave_comp(p), p, col), device_id_type=MESH,
        )

    def arrived(s):
        return pltpu.make_async_remote_copy(
            src_ref=send_v.at[s], dst_ref=recv_v.at[s], send_sem=send_sem.at[s], recv_sem=recv_sem.at[s],
            device_id=(0, s, col), device_id_type=MESH,
        )

    def back_copy(p):
        return pltpu.make_async_remote_copy(
            src_ref=back_v.at[p], dst_ref=home_v.at[me], send_sem=back_send_sem.at[p],
            recv_sem=back_recv_sem.at[me], device_id=(0, p, col), device_id_type=MESH,
        )

    def back_arrived(s):
        return pltpu.make_async_remote_copy(
            src_ref=back_v.at[s], dst_ref=home_v.at[s], send_sem=back_send_sem.at[s],
            recv_sem=back_recv_sem.at[s], device_id=(0, s, col), device_id_type=MESH,
        )

    def take_home(m):
        back_arrived(m).wait_recv()
        new_state[pl.ds(m, LAT, stride=WAVES), :] = home_v[m].astype(F32)

    def elsewhere(r):
        return jnp.logical_not(jnp.logical_and(works, jnp.logical_and(air, r == me)))

    @pl.when(air)
    def _():
        load_gauss.wait()
        for r in range(LAT):
            weight_v[r : r + 1, :] = jnp.full((1, COLS), gauss_s[r], F32)
        load_surface.wait()
        load_state.wait()
        pl.semaphore_wait(barrier, ROWS)

        @pl.when(early)
        def _():
            greet(0, 0, col)

        weights = weight_v[...]

        for s in range(ROWS - 1):
            p = far_partner(me, s)
            send_v[p] = (x_v[pl.ds(p, LAT, stride=WAVES), :] * weights).astype(BF16)
            out_copy(p).start()

        own = (x_v[pl.ds(me, LAT, stride=WAVES), :] * weights).astype(BF16)

        @pl.when(late)
        def _():
            send_v[me] = own
            out_copy(me).start()
            greet(1, me, col)

            for s in range(ROWS - 1):
                greet(0, far_partner(me, s), col)

        @pl.when(jnp.logical_not(late))
        def _():
            recv_v[me] = own

        pair_copy.start()

    @pl.when(jnp.logical_not(air))
    def _():
        load_mixing.start()
        load_surface.wait()
        total = sum(there.astype(jnp.int32) for there in has)
        load_counts.wait()
        for r in range(LAT):
            mask_v[r * WAVES : (r + 1) * WAVES, :] = jnp.broadcast_to((lane < count_s[r]).astype(F32), (WAVES, COLS))
        load_mixing.wait()
        pick = (lax.broadcasted_iota(jnp.int32, (CHUNK, WAVES), 0) & (WAVES - 1)) == lax.broadcasted_iota(
            jnp.int32, (CHUNK, WAVES), 1
        )
        pick = pick.astype(F32)
        tall = jnp.dot(pick, mix_v[...], precision=lax.Precision.HIGHEST, preferred_element_type=F32)
        wide = lax.dot_general(
            tall, pick, (((1,), (1,)), ((), ())), precision=lax.Precision.HIGHEST, preferred_element_type=F32
        )
        same = (lax.broadcasted_iota(jnp.int32, (CHUNK, CHUNK), 0) >> 5) == (
            lax.broadcasted_iota(jnp.int32, (CHUNK, CHUNK), 1) >> 5
        )
        block_v[...] = jnp.where(same, wide, 0.0)
        load_state.wait()
        for i in range(CHUNKS):
            part = slice(i * CHUNK, (i + 1) * CHUNK)
            mixed = jnp.dot(block_v[...], x_v[part, :], precision=lax.Precision.HIGHEST, preferred_element_type=F32)
            new_state[part, :] = x_v[part, :] + mask_v[part, :] * mixed
        pl.semaphore_wait(barrier, total + jnp.where(helper, ROWS - 1, 1))

        @pl.when(helper)
        def _():
            greet(0, 0, col)

        @pl.when(jnp.logical_not(helper))
        def _():
            pair_copy.start()

        def halo_copy(sweep, side):
            u = u_v.at[sweep]
            if side == 0:
                src, dst = u.at[pl.ds(WAVES, WAVES)], u.at[pl.ds(CELLS + WAVES, WAVES)]
            elif side == 1:
                src, dst = u.at[pl.ds(CELLS, WAVES)], u.at[pl.ds(0, WAVES)]
            else:
                src, dst = edge_v.at[sweep, side - 2], side_v.at[sweep, 3 - side]
            return pltpu.make_async_remote_copy(
                src_ref=src, dst_ref=dst, send_sem=halo_send.at[sweep, side], recv_sem=halo_recv.at[sweep, side ^ 1],
                device_id=beside[side], device_id_type=MESH,
            )

        def halo_arrived(sweep, side):
            u = u_v.at[sweep]
            if side == 0:
                dst = u.at[pl.ds(0, WAVES)]
            elif side == 1:
                dst = u.at[pl.ds(CELLS + WAVES, WAVES)]
            else:
                dst = side_v.at[sweep, side - 2]
            return pltpu.make_async_remote_copy(
                src_ref=dst, dst_ref=dst, send_sem=halo_send.at[sweep, side], recv_sem=halo_recv.at[sweep, side],
                device_id=(1, me, col), device_id_type=MESH,
            )

        for sweep in range(2):
            for i in range(CELLS // COLS):
                part = slice(i * COLS, (i + 1) * COLS)
                u = mask_v[part, :] * new_state[part, :]
                u_v[sweep, WAVES + i * COLS : WAVES + (i + 1) * COLS, :] = u
                flipped = u.T
                edge_v[sweep, 0, i : i + 1, :] = flipped[0:1, :]
                edge_v[sweep, 1, i : i + 1, :] = flipped[COLS - 1 : COLS, :]
            for side in range(4):
                @pl.when(has[side])
                def _():
                    halo_copy(sweep, side).start()

                @pl.when(jnp.logical_not(has[side]))
                def _():
                    if side == 0:
                        u_v[sweep, 0:WAVES, :] = jnp.zeros((WAVES, COLS), F32)
                    elif side == 1:
                        u_v[sweep, CELLS + WAVES : CELLS + 2 * WAVES, :] = jnp.zeros((WAVES, COLS), F32)
                    else:
                        side_v[sweep, side - 2] = jnp.zeros((16, COLS), F32)

            for side in range(4):
                @pl.when(has[side])
                def _():
                    halo_arrived(sweep, side).wait_recv()

            west = side_v[sweep, 0].T
            east = side_v[sweep, 1].T
            for i in range(CELLS // COLS):
                part = slice(i * COLS, (i + 1) * COLS)
                low = i * COLS
                centre = u_v[sweep, low + WAVES : low + WAVES + COLS, :]
                left = jnp.where(lane == 0, west[:, i : i + 1], pltpu.roll(centre, 1, 1))
                right = jnp.where(lane == COLS - 1, east[:, i : i + 1], pltpu.roll(centre, COLS - 1, 1))
                above = u_v[sweep, low : low + COLS, :]
                below = u_v[sweep, low + 2 * WAVES : low + 2 * WAVES + COLS, :]
                laplace = above + below + left + right - 4.0 * centre
                new_state[part, :] = new_state[part, :] + STEP * mask_v[part, :] * laplace
        for sweep in range(2):
            for side in range(4):
                @pl.when(has[side])
                def _():
                    halo_copy(sweep, side).wait_send()

    @pl.when(works)
    def _():
        n = (lax.broadcasted_iota(jnp.int32, (1, NWAVE), 1) + me).astype(F32)
        ratio = n * (n + 1.0) / (1279.0 * 1280.0)
        damp_v[...] = 1.0 / (1.0 + 20.0 * ratio * ratio)
        load_legendre.wait()

        seen = set()
        for place, j in enumerate(CHUNK_ORDER):
            if place == CHUNKS - 1:

                @pl.when(early)
                def _():
                    pl.semaphore_wait(barrier, 1)

                @pl.when(helper)
                def _():
                    pair_copy.start()

            for s in range(CHUNK * j // LAT, (CHUNK * (j + 1) - 1) // LAT + 1):
                if s in seen:
                    continue
                seen.add(s)

                @pl.when(elsewhere(s))
                def _():
                    arrived(s).wait_recv()

                lat_v[s * LAT : (s + 1) * LAT, :] = recv_v[s].astype(F32)
            part = lat_v[j * CHUNK : (j + 1) * CHUNK, :].T.astype(BF16)
            product = jnp.dot(part, leg_v[j * CHUNK : (j + 1) * CHUNK, :], preferred_element_type=F32)
            if place == 0:
                acc_v[...] = product
            elif place < CHUNKS - 1:
                acc_v[...] += product
            else:
                filt_v[...] = (damp_v[...] * (acc_v[...] + product)).T.astype(BF16)

        for k in range(4):
            quarter = (me >> 3) ^ (3, 2, 1, 0)[k]
            block = jnp.dot(
                leg_v[pl.ds(pl.multiple_of(quarter * (8 * LAT), 8 * LAT), 8 * LAT), :], filt_v[...],
                preferred_element_type=F32,
            )
            for j in range(8):
                p = quarter * 8 + j
                back_v[p] = block[j * LAT : (j + 1) * LAT, :].astype(BF16)
                if k < 3:
                    back_copy(p).start()
                else:

                    @pl.when(elsewhere(p))
                    def _():
                        back_copy(p).start()

        @pl.when(air)
        def _():
            home_v[me] = back_v[me]

    @pl.when(air)
    def _():
        load_counts.wait()
        load_source.wait()
        surface_step(0.5)

        for s in range(ROWS - 1):
            out_copy(far_partner(me, s)).wait_send()

        @pl.when(late)
        def _():
            out_copy(me).wait_send()
            take_home(me)

        @pl.when(jnp.logical_not(late))
        def _():
            new_state[pl.ds(me, LAT, stride=WAVES), :] = home_v[me].astype(F32)

        pair_copy.wait_send()
        for s in range(ROWS - 2, 8, -1):
            take_home(far_partner(me, s))

    @pl.when(works)
    def _():
        for s in range(ROWS - 1):
            back_copy(far_partner(me, s)).wait_send()

        @pl.when(helper)
        def _():
            back_copy(me).wait_send()

    @pl.when(air)
    def _():
        for s in range(8, -1, -1):
            take_home(far_partner(me, s))

    @pl.when(jnp.logical_not(air))
    def _():
        load_source.wait()
        surface_step(0.25)
        new_state[pl.ds(0, LAT, stride=WAVES), :] = new_state[pl.ds(0, LAT, stride=WAVES), :] + 0.3 * gap_v[...]
        load_gauss.wait()
        pair_copy.wait_send()


def save(state, surface, new_state, new_surface, sem):
    part = CELLS // SAVES
    copies = [
        pltpu.make_async_copy(
            state.at[pl.ds(i * part, part)], new_state.at[pl.ds(i * part, part)], sem.at[i]
        )
        for i in range(SAVES)
    ]
    copies.append(pltpu.make_async_copy(surface, new_surface, sem.at[SAVES]))
    for copy in copies:
        copy.start()
    for copy in copies:
        copy.wait()


def shards(model_state, legendre, gauss_weight, mixing, surface, sea_count, remap_source):
    anywhere = pl.BlockSpec(memory_space=pl.ANY)
    vmem = pltpu.VMEM
    dma = pltpu.SemaphoreType.DMA
    new_state, new_surface = pl.pallas_call(
        kernel,
        out_shape=(
            pltpu.VMEM((CELLS, COLS), F32),
            pltpu.VMEM((LAT, COLS), F32),
        ),
        in_specs=[anywhere] * 7,
        out_specs=(pl.BlockSpec(memory_space=vmem),) * 2,
        scratch_shapes=[
            vmem((CELLS, COLS), F32),
            vmem((NWAVE, NWAVE), BF16),
            pltpu.SMEM((LAT,), F32),
            vmem((WAVES, WAVES), F32),
            vmem((LAT, COLS), F32),
            pltpu.SMEM((LAT,), jnp.int32),
            vmem((LAT, COLS), jnp.int32),
            vmem((LAT, COLS), F32),
            vmem((LAT, COLS), F32),
            vmem((ROWS, LAT, COLS), BF16),
            vmem((ROWS, LAT, COLS), BF16),
            vmem((NWAVE, COLS), F32),
            vmem((COLS, NWAVE), F32),
            vmem((1, NWAVE), F32),
            vmem((NWAVE, COLS), BF16),
            vmem((ROWS, LAT, COLS), BF16),
            vmem((ROWS, LAT, COLS), BF16),
            vmem((CELLS, COLS), F32),
            vmem((CHUNK, CHUNK), F32),
            vmem((2, CELLS + 2 * WAVES, COLS), F32),
            vmem((2, 2, 16, COLS), F32),
            vmem((2, 2, 16, COLS), F32),
            vmem((LAT, COLS), F32),
            dma((7,)), dma((ROWS,)), dma((ROWS,)), dma((ROWS,)), dma((ROWS,)), dma((2,)),
            dma((2, 4)), dma((2, 4)),
        ],
        compiler_params=pltpu.CompilerParams(
            collective_id=0, has_side_effects=True, vmem_limit_bytes=48 * 1024 * 1024
        ),
        cost_estimate=pl.CostEstimate(flops=900_000_000, bytes_accessed=5_000_000, transcendentals=0),
    )(
        *(
            pltpu.with_memory_space_constraint(operand, pltpu.HBM)
            for operand in (
                model_state.reshape(CELLS, COLS),
                legendre.reshape(NWAVE, NWAVE),
                gauss_weight,
                mixing,
                surface.reshape(LAT, COLS),
                sea_count.reshape(LAT),
                remap_source.reshape(LAT, COLS),
            )
        )
    )
    new_state, new_surface = pl.pallas_call(
        save,
        out_shape=(
            pltpu.HBM((CELLS, COLS), F32),
            pltpu.HBM((LAT, COLS), F32),
        ),
        in_specs=[anywhere] * 2,
        out_specs=(anywhere,) * 2,
        scratch_shapes=[dma((SAVES + 1,))],
    )(
        pltpu.with_memory_space_constraint(new_state, pltpu.VMEM),
        pltpu.with_memory_space_constraint(new_surface, pltpu.VMEM),
    )
    return new_state.reshape(1, LAT, WAVES, COLS), new_surface.reshape(1, LAT, COLS)


def solution(mesh):
    in_specs = (
        P("comp", "row", None, "col"),
        P("row", None, None),
        P("row"),
        P(),
        P("comp", "row", "col"),
        P("comp", "row", "col"),
        P("comp", "row", "col"),
    )
    out_specs = (P("comp", "row", None, "col"), P("comp", "row", "col"))
    return jax.shard_map(shards, mesh=mesh, in_specs=in_specs, out_specs=out_specs, check_vma=False)
```

```python
import functools

import jax
import jax.numpy as jnp
from jax import lax
from jax.experimental import pallas as pl
from jax.experimental.pallas import tpu as pltpu
from jax.sharding import PartitionSpec as P

MESH = pl.DeviceIdType.MESH
F32 = jnp.float32
BF16 = jnp.bfloat16

ROWS = 32
LAT = 40
WAVES = 32
COLS = 128
NWAVE = 1280
CELLS = LAT * WAVES
CHUNK = 256
CHUNKS = NWAVE // CHUNK
CHUNK_ORDER = (2, 4, 3, 1, 0)
STEP = 0.2
SAVES = 4


def far_partner(me, step):
    ring, inner = step // 4, step % 4
    shift = (8 - ring) // 2 if ring % 2 else 8 - (8 - ring) // 2
    flip = (1 - inner // 2) * 16 + (1 - inner % 2)
    return ((me & 17) ^ flip) + ((me + 2 * shift) & 14)


def kernel(
    state, legendre, gauss, mixing, surface, counts, source,
    new_state, new_surface,
    x_v, leg_v, gauss_s, mix_v, surf_v, count_s, source_v, partner_v,
    weight_v, send_v, recv_v, lat_v, acc_v, damp_v, filt_v, back_v, home_v,
    mask_v, block_v, u_v, edge_v, side_v, gap_v,
    in_sem, send_sem, recv_sem, back_send_sem, back_recv_sem, pair_sem, halo_send, halo_recv,
):
    comp = lax.axis_index("comp")
    me = lax.axis_index("row")
    col = lax.axis_index("col")
    n_col = lax.axis_size("col")
    air = comp == 0

    barrier = pltpu.get_barrier_semaphore()

    def greet(c, r, k):
        pl.semaphore_signal(barrier, inc=1, device_id=(c, r, k), device_id_type=MESH)

    loads = [
        pltpu.make_async_copy(src, dst, in_sem.at[i])
        for i, (src, dst) in enumerate(
            [(state, x_v), (gauss, gauss_s), (counts, count_s), (surface, surf_v), (source, source_v),
             (legendre, leg_v), (mixing, mix_v)]
        )
    ]
    load_state, load_gauss, load_counts, load_surface, load_source, load_legendre, load_mixing = loads

    for load in (load_gauss, load_state, load_surface, load_counts, load_source):
        load.start()

    staged = col == 0
    late = jnp.logical_and(jnp.logical_and(staged, me == 0), air)
    helper = jnp.logical_and(jnp.logical_and(staged, me == 0), jnp.logical_not(air))
    early = jnp.logical_or(jnp.logical_and(jnp.logical_and(staged, me > 0), air), helper)
    works = jnp.logical_or(jnp.logical_and(air, jnp.logical_not(late)), helper)

    def wave_comp(p):
        return jnp.where(jnp.logical_and(staged, p == 0), 1, 0)

    @pl.when(jnp.logical_not(jnp.logical_or(late, helper)))
    def _():
        greet(1 - comp, me, col)

    @pl.when(works)
    def _():
        for s in range(ROWS - 1):
            p = far_partner(me, s)
            greet(wave_comp(p), p, col)

    has = [me > 0, me < ROWS - 1, col > 0, col < n_col - 1]
    beside = [(1, me - 1, col), (1, me + 1, col), (1, me, col - 1), (1, me, col + 1)]

    @pl.when(jnp.logical_not(air))
    def _():
        for there, place in zip(has, beside):
            @pl.when(there)
            def _():
                greet(*place)

    @pl.when(works)
    def _():
        load_legendre.start()

    @pl.when(late)
    def _():
        pl.semaphore_wait(barrier, ROWS)
        for s in range(ROWS - 1):
            greet(0, far_partner(me, s), col)
        greet(1, me, col)

    pair_copy = pltpu.make_async_remote_copy(
        src_ref=surf_v, dst_ref=partner_v, send_sem=pair_sem.at[0], recv_sem=pair_sem.at[1],
        device_id=(1 - comp, me, col), device_id_type=MESH,
    )

    lane = lax.broadcasted_iota(jnp.int32, (1, COLS), 1)

    def surface_step(rate):
        pair_copy.wait_recv()
        for r in range(LAT):
            gap_v[r : r + 1, :] = (lane < count_s[r]).astype(F32)
        where_row = source_v[...] >> 7
        where_lane = source_v[...] & 127

        def one(r, total):
            row = jnp.broadcast_to(partner_v[pl.ds(r, 1), :], (LAT, COLS))
            got = jnp.take_along_axis(row, where_lane, axis=1)
            return jnp.where(where_row == r, got, total)

        pulled = lax.fori_loop(0, LAT, one, jnp.zeros((LAT, COLS), F32))
        gap = gap_v[...] * (pulled - surf_v[...])
        gap_v[...] = gap
        new_surface[...] = surf_v[...] + rate * gap

    def out_copy(p):
        return pltpu.make_async_remote_copy(
            src_ref=send_v.at[p], dst_ref=recv_v.at[me], send_sem=send_sem.at[p], recv_sem=recv_sem.at[me],
            device_id=(wave_comp(p), p, col), device_id_type=MESH,
        )

    def arrived(s):
        return pltpu.make_async_remote_copy(
            src_ref=send_v.at[s], dst_ref=recv_v.at[s], send_sem=send_sem.at[s], recv_sem=recv_sem.at[s],
            device_id=(0, s, col), device_id_type=MESH,
        )

    def back_copy(p):
        return pltpu.make_async_remote_copy(
            src_ref=back_v.at[p], dst_ref=home_v.at[me], send_sem=back_send_sem.at[p],
            recv_sem=back_recv_sem.at[me], device_id=(0, p, col), device_id_type=MESH,
        )

    def back_arrived(s):
        return pltpu.make_async_remote_copy(
            src_ref=back_v.at[s], dst_ref=home_v.at[s], send_sem=back_send_sem.at[s],
            recv_sem=back_recv_sem.at[s], device_id=(0, s, col), device_id_type=MESH,
        )

    def take_home(m):
        back_arrived(m).wait_recv()
        new_state[pl.ds(m, LAT, stride=WAVES), :] = home_v[m].astype(F32)

    def elsewhere(r):
        return jnp.logical_not(jnp.logical_and(works, jnp.logical_and(air, r == me)))

    @pl.when(air)
    def _():
        load_gauss.wait()
        for r in range(LAT):
            weight_v[r : r + 1, :] = jnp.full((1, COLS), gauss_s[r], F32)
        load_state.wait()
        @pl.when(jnp.logical_not(late))
        def _():
            pl.semaphore_wait(barrier, ROWS)

        @pl.when(early)
        def _():
            greet(0, 0, col)

        weights = weight_v[...]

        for s in range(ROWS - 1):
            p = far_partner(me, s)
            send_v[p] = (x_v[pl.ds(p, LAT, stride=WAVES), :] * weights).astype(BF16)
            out_copy(p).start()

        own = (x_v[pl.ds(me, LAT, stride=WAVES), :] * weights).astype(BF16)

        @pl.when(late)
        def _():
            send_v[me] = own
            out_copy(me).start()

        @pl.when(jnp.logical_not(late))
        def _():
            recv_v[me] = own

        load_surface.wait()
        pair_copy.start()

    @pl.when(jnp.logical_not(air))
    def _():
        load_mixing.start()
        load_surface.wait()
        total = sum(there.astype(jnp.int32) for there in has)
        load_counts.wait()
        for r in range(LAT):
            mask_v[r * WAVES : (r + 1) * WAVES, :] = jnp.broadcast_to((lane < count_s[r]).astype(F32), (WAVES, COLS))
        load_mixing.wait()
        pick = (lax.broadcasted_iota(jnp.int32, (CHUNK, WAVES), 0) & (WAVES - 1)) == lax.broadcasted_iota(
            jnp.int32, (CHUNK, WAVES), 1
        )
        pick = pick.astype(F32)
        tall = jnp.dot(pick, mix_v[...], precision=lax.Precision.HIGHEST, preferred_element_type=F32)
        wide = lax.dot_general(
            tall, pick, (((1,), (1,)), ((), ())), precision=lax.Precision.HIGHEST, preferred_element_type=F32
        )
        same = (lax.broadcasted_iota(jnp.int32, (CHUNK, CHUNK), 0) >> 5) == (
            lax.broadcasted_iota(jnp.int32, (CHUNK, CHUNK), 1) >> 5
        )
        block_v[...] = jnp.where(same, wide, 0.0)
        load_state.wait()
        for i in range(CHUNKS):
            part = slice(i * CHUNK, (i + 1) * CHUNK)
            mixed = jnp.dot(block_v[...], x_v[part, :], precision=lax.Precision.HIGHEST, preferred_element_type=F32)
            new_state[part, :] = x_v[part, :] + mask_v[part, :] * mixed
        pl.semaphore_wait(barrier, total + jnp.where(helper, ROWS - 1, 1))

        @pl.when(helper)
        def _():
            greet(0, 0, col)

        @pl.when(jnp.logical_not(helper))
        def _():
            pair_copy.start()

        def halo_copy(sweep, side):
            u = u_v.at[sweep]
            if side == 0:
                src, dst = u.at[pl.ds(WAVES, WAVES)], u.at[pl.ds(CELLS + WAVES, WAVES)]
            elif side == 1:
                src, dst = u.at[pl.ds(CELLS, WAVES)], u.at[pl.ds(0, WAVES)]
            else:
                src, dst = edge_v.at[sweep, side - 2], side_v.at[sweep, 3 - side]
            return pltpu.make_async_remote_copy(
                src_ref=src, dst_ref=dst, send_sem=halo_send.at[sweep, side], recv_sem=halo_recv.at[sweep, side ^ 1],
                device_id=beside[side], device_id_type=MESH,
            )

        def halo_arrived(sweep, side):
            u = u_v.at[sweep]
            if side == 0:
                dst = u.at[pl.ds(0, WAVES)]
            elif side == 1:
                dst = u.at[pl.ds(CELLS + WAVES, WAVES)]
            else:
                dst = side_v.at[sweep, side - 2]
            return pltpu.make_async_remote_copy(
                src_ref=dst, dst_ref=dst, send_sem=halo_send.at[sweep, side], recv_sem=halo_recv.at[sweep, side],
                device_id=(1, me, col), device_id_type=MESH,
            )

        for sweep in range(2):
            for i in range(CELLS // COLS):
                part = slice(i * COLS, (i + 1) * COLS)
                u = mask_v[part, :] * new_state[part, :]
                u_v[sweep, WAVES + i * COLS : WAVES + (i + 1) * COLS, :] = u
                flipped = u.T
                edge_v[sweep, 0, i : i + 1, :] = flipped[0:1, :]
                edge_v[sweep, 1, i : i + 1, :] = flipped[COLS - 1 : COLS, :]
            for side in range(4):
                @pl.when(has[side])
                def _():
                    halo_copy(sweep, side).start()

                @pl.when(jnp.logical_not(has[side]))
                def _():
                    if side == 0:
                        u_v[sweep, 0:WAVES, :] = jnp.zeros((WAVES, COLS), F32)
                    elif side == 1:
                        u_v[sweep, CELLS + WAVES : CELLS + 2 * WAVES, :] = jnp.zeros((WAVES, COLS), F32)
                    else:
                        side_v[sweep, side - 2] = jnp.zeros((16, COLS), F32)

            for side in range(4):
                @pl.when(has[side])
                def _():
                    halo_arrived(sweep, side).wait_recv()

            west = side_v[sweep, 0].T
            east = side_v[sweep, 1].T
            for i in range(CELLS // COLS):
                part = slice(i * COLS, (i + 1) * COLS)
                low = i * COLS
                centre = u_v[sweep, low + WAVES : low + WAVES + COLS, :]
                left = jnp.where(lane == 0, west[:, i : i + 1], pltpu.roll(centre, 1, 1))
                right = jnp.where(lane == COLS - 1, east[:, i : i + 1], pltpu.roll(centre, COLS - 1, 1))
                above = u_v[sweep, low : low + COLS, :]
                below = u_v[sweep, low + 2 * WAVES : low + 2 * WAVES + COLS, :]
                laplace = above + below + left + right - 4.0 * centre
                new_state[part, :] = new_state[part, :] + STEP * mask_v[part, :] * laplace
        for sweep in range(2):
            for side in range(4):
                @pl.when(has[side])
                def _():
                    halo_copy(sweep, side).wait_send()

    @pl.when(works)
    def _():
        n = (lax.broadcasted_iota(jnp.int32, (1, NWAVE), 1) + me).astype(F32)
        ratio = n * (n + 1.0) / (1279.0 * 1280.0)
        damp_v[...] = 1.0 / (1.0 + 20.0 * ratio * ratio)
        load_legendre.wait()

        seen = set()
        for place, j in enumerate(CHUNK_ORDER):
            if place == CHUNKS - 1:

                @pl.when(early)
                def _():
                    pl.semaphore_wait(barrier, 1)

                @pl.when(helper)
                def _():
                    pair_copy.start()

            for s in range((CHUNK * (j + 1) - 1) // LAT, CHUNK * j // LAT - 1, -1):
                if s in seen:
                    continue
                seen.add(s)

                @pl.when(elsewhere(s))
                def _():
                    arrived(s).wait_recv()

                lat_v[s * LAT : (s + 1) * LAT, :] = recv_v[s].astype(F32)
            part = lat_v[j * CHUNK : (j + 1) * CHUNK, :].T.astype(BF16)
            product = jnp.dot(part, leg_v[j * CHUNK : (j + 1) * CHUNK, :], preferred_element_type=F32)
            if place == 0:
                acc_v[...] = product
            elif place < CHUNKS - 1:
                acc_v[...] += product
            else:
                filt_v[...] = (damp_v[...] * (acc_v[...] + product)).T.astype(BF16)

        for k in range(4):
            quarter = (me >> 3) ^ (3, 2, 1, 0)[k]
            block = jnp.dot(
                leg_v[pl.ds(pl.multiple_of(quarter * (8 * LAT), 8 * LAT), 8 * LAT), :], filt_v[...],
                preferred_element_type=F32,
            )
            for j in range(8):
                p = quarter * 8 + j
                back_v[p] = block[j * LAT : (j + 1) * LAT, :].astype(BF16)
                if k < 3:
                    back_copy(p).start()
                else:

                    @pl.when(elsewhere(p))
                    def _():
                        back_copy(p).start()

        @pl.when(air)
        def _():
            home_v[me] = back_v[me]

    @pl.when(air)
    def _():
        load_counts.wait()
        load_source.wait()
        surface_step(0.5)

        for s in range(ROWS - 1):
            out_copy(far_partner(me, s)).wait_send()

        @pl.when(late)
        def _():
            out_copy(me).wait_send()
            take_home(me)

        @pl.when(jnp.logical_not(late))
        def _():
            new_state[pl.ds(me, LAT, stride=WAVES), :] = home_v[me].astype(F32)

        pair_copy.wait_send()
        for s in range(ROWS - 2, 8, -1):
            take_home(far_partner(me, s))

    @pl.when(works)
    def _():
        for s in range(ROWS - 1):
            back_copy(far_partner(me, s)).wait_send()

        @pl.when(helper)
        def _():
            back_copy(me).wait_send()

    @pl.when(air)
    def _():
        for s in range(8, -1, -1):
            take_home(far_partner(me, s))

    @pl.when(jnp.logical_not(air))
    def _():
        load_source.wait()
        surface_step(0.25)
        new_state[pl.ds(0, LAT, stride=WAVES), :] = new_state[pl.ds(0, LAT, stride=WAVES), :] + 0.3 * gap_v[...]
        load_gauss.wait()
        pair_copy.wait_send()


def save(state, surface, new_state, new_surface, sem):
    part = CELLS // SAVES
    copies = [
        pltpu.make_async_copy(
            state.at[pl.ds(i * part, part)], new_state.at[pl.ds(i * part, part)], sem.at[i]
        )
        for i in range(SAVES)
    ]
    copies.append(pltpu.make_async_copy(surface, new_surface, sem.at[SAVES]))
    for copy in copies:
        copy.start()
    for copy in copies:
        copy.wait()


def shards(model_state, legendre, gauss_weight, mixing, surface, sea_count, remap_source):
    anywhere = pl.BlockSpec(memory_space=pl.ANY)
    vmem = pltpu.VMEM
    dma = pltpu.SemaphoreType.DMA
    new_state, new_surface = pl.pallas_call(
        kernel,
        out_shape=(
            pltpu.VMEM((CELLS, COLS), F32),
            pltpu.VMEM((LAT, COLS), F32),
        ),
        in_specs=[anywhere] * 7,
        out_specs=(pl.BlockSpec(memory_space=vmem),) * 2,
        scratch_shapes=[
            vmem((CELLS, COLS), F32),
            vmem((NWAVE, NWAVE), BF16),
            pltpu.SMEM((LAT,), F32),
            vmem((WAVES, WAVES), F32),
            vmem((LAT, COLS), F32),
            pltpu.SMEM((LAT,), jnp.int32),
            vmem((LAT, COLS), jnp.int32),
            vmem((LAT, COLS), F32),
            vmem((LAT, COLS), F32),
            vmem((ROWS, LAT, COLS), BF16),
            vmem((ROWS, LAT, COLS), BF16),
            vmem((NWAVE, COLS), F32),
            vmem((COLS, NWAVE), F32),
            vmem((1, NWAVE), F32),
            vmem((NWAVE, COLS), BF16),
            vmem((ROWS, LAT, COLS), BF16),
            vmem((ROWS, LAT, COLS), BF16),
            vmem((CELLS, COLS), F32),
            vmem((CHUNK, CHUNK), F32),
            vmem((2, CELLS + 2 * WAVES, COLS), F32),
            vmem((2, 2, 16, COLS), F32),
            vmem((2, 2, 16, COLS), F32),
            vmem((LAT, COLS), F32),
            dma((7,)), dma((ROWS,)), dma((ROWS,)), dma((ROWS,)), dma((ROWS,)), dma((2,)),
            dma((2, 4)), dma((2, 4)),
        ],
        compiler_params=pltpu.CompilerParams(
            collective_id=0, has_side_effects=True, vmem_limit_bytes=48 * 1024 * 1024
        ),
        cost_estimate=pl.CostEstimate(flops=900_000_000, bytes_accessed=5_000_000, transcendentals=0),
    )(
        *(
            pltpu.with_memory_space_constraint(operand, pltpu.HBM)
            for operand in (
                model_state.reshape(CELLS, COLS),
                legendre.reshape(NWAVE, NWAVE),
                gauss_weight,
                mixing,
                surface.reshape(LAT, COLS),
                sea_count.reshape(LAT),
                remap_source.reshape(LAT, COLS),
            )
        )
    )
    new_state, new_surface = pl.pallas_call(
        save,
        out_shape=(
            pltpu.HBM((CELLS, COLS), F32),
            pltpu.HBM((LAT, COLS), F32),
        ),
        in_specs=[anywhere] * 2,
        out_specs=(anywhere,) * 2,
        scratch_shapes=[dma((SAVES + 1,))],
    )(
        pltpu.with_memory_space_constraint(new_state, pltpu.VMEM),
        pltpu.with_memory_space_constraint(new_surface, pltpu.VMEM),
    )
    return new_state.reshape(1, LAT, WAVES, COLS), new_surface.reshape(1, LAT, COLS)


def solution(mesh):
    in_specs = (
        P("comp", "row", None, "col"),
        P("row", None, None),
        P("row"),
        P(),
        P("comp", "row", "col"),
        P("comp", "row", "col"),
        P("comp", "row", "col"),
    )
    out_specs = (P("comp", "row", None, "col"), P("comp", "row", "col"))
    return jax.shard_map(shards, mesh=mesh, in_specs=in_specs, out_specs=out_specs, check_vma=False)
```
